256 devices in a mesh: wave: 64 (over z, x, core), lev: 4 (over y).
Axes of the slice: x: 4, y: 4, z: 8, core: 2. Of those that a mesh axis runs over, the one named last changes fastest.
Arguments:
- coeffs: bfloat16 [1280, 192, 1280], P('wave', 'lev'), may hold values from -0.3125 to 0.3125
- legendre: bfloat16 [1280, 64, 1280], P('wave'), may hold values from -0.15625 to 0.15625
- wave_of_slot: int32 [1280], replicated, may hold values from 0 to 1279, each once
- lon_count: int32 [64], P('wave'), may hold values from 1280 to 5120, as said below
Outputs:
- grid_field: bfloat16 [96, 64, 5120], P(None, 'wave', 'lev')
The draws below stay inside these ranges and needn't reach their ends.
Inputs may be any that keep to these rules, and one draw needn't show every extreme that they name: `lon_count`: each count is a multiple of 4; some latitude has exactly 5120.
All inputs are finite; a program needn't handle non-finite values.
Results may differ from the reference program's by a relative error of at most 0.0055.
Values may be sent and summed in bfloat16 or wider, within the bound.
A program may use at most 192 MiB of HBM per device.

```python
import math
import jax
import jax.numpy as jnp
from jax import lax

M = 1280
NLONMAX = 5120
LEV = 32
LATITUDES = 64


def draw_lon_count(key, part):
    key_one, key_two = jax.random.split(key)
    quarters = jax.random.randint(key_one, (LATITUDES,), NLONMAX // 16, NLONMAX // 4 + 1)
    widest = jax.random.randint(key_two, (), 0, LATITUDES)
    quarters = jnp.where(jnp.arange(LATITUDES) == widest, NLONMAX // 4, quarters)
    return (4 * quarters).astype(jnp.int32)


def steps_of(rng, shape, cuts, low, top_value):
    def one(axis_at, blocks):
        draws = jax.random.uniform(jax.random.fold_in(jax.random.fold_in(rng, 6), axis_at), (blocks,), jnp.float32, low / len(cuts), top_value / len(cuts))
        return jnp.repeat(jnp.exp(draws), shape[axis_at] // blocks).reshape((-1,) + (1,) * (len(shape) - axis_at - 1))

    loudness = one(*cuts[0])
    for cut in cuts[1:]:
        loudness = loudness * one(*cut)
    return loudness


def gaussian(own_key, shape, width, most, shards=(), kind=jnp.bfloat16):
    entries = width * jax.random.normal(own_key, shape, jnp.float32)
    if shards:
        entries = entries * steps_of(own_key, shape, shards, -0.22, 0.18)
    return jnp.clip(entries, -most, most).astype(kind)


def setup_inputs(seed: int = 0) -> dict:
    key_of = jax.random.split(jax.random.key(seed), 5)
    return {
        "coeffs": gaussian(key_of[0], (M, 6 * LEV, M), 0.02, 0.3125, ((0, 64), (1, 4))),
        "legendre": gaussian(key_of[1], (M, LATITUDES, M), M ** -0.5, 0.15625, ((0, 64),)),
        "wave_of_slot": jax.random.permutation(key_of[2], M).astype(jnp.int32),
        "lon_count": draw_lon_count(jax.random.fold_in(key_of[4], 71), 0),
    }


TWO_PI = 2.0 * math.pi
FINE_SPAN = 64


def fourier_table(wavenum, lon_total, lon_start, tile_width):
    column = wavenum.astype(jnp.int32)[:, None]
    coarse_count = tile_width // FINE_SPAN
    coarse_index = lon_start + FINE_SPAN * lax.iota(jnp.int32, coarse_count)[None, :]
    fine_index = lax.iota(jnp.int32, FINE_SPAN)[None, :]
    step_angle = TWO_PI / lon_total.astype(jnp.float32)
    coarse_angle = ((column * coarse_index) % lon_total).astype(jnp.float32) * step_angle
    fine_angle = ((column * fine_index) % lon_total).astype(jnp.float32) * step_angle
    cos_coarse = jnp.cos(coarse_angle)[:, :, None]
    sin_coarse = jnp.sin(coarse_angle)[:, :, None]
    cos_fine = jnp.cos(fine_angle)[:, None, :]
    sin_fine = jnp.sin(fine_angle)[:, None, :]
    cos_sum = (cos_coarse * cos_fine - sin_coarse * sin_fine).reshape(column.shape[0], tile_width)
    sin_sum = (sin_coarse * cos_fine + cos_coarse * sin_fine).reshape(column.shape[0], tile_width)
    lon_index = lon_start + lax.iota(jnp.int32, tile_width)[None, :]
    kept_mask = (2 * column <= lon_total - 1) & (lon_index < lon_total)
    weight = jnp.where(column == 0, jnp.float32(1.0), jnp.float32(2.0))
    factor = jnp.where(kept_mask, weight, jnp.float32(0.0))
    cos_part = (factor * cos_sum).astype(jnp.bfloat16)
    sin_part = (-factor * sin_sum).astype(jnp.bfloat16)
    return jnp.stack([cos_part, sin_part])


def reference(coeffs, legendre, wave_of_slot, lon_count):
    degree_off = lax.iota(jnp.int32, M)
    valid_mask = degree_off[None, :] < (M - wave_of_slot)[:, None]
    masked = coeffs * valid_mask[:, None, :].astype(coeffs.dtype)

    def legendre_slot(operands):
        values, spectra = operands
        return jnp.dot(values, spectra.T, preferred_element_type=jnp.float32).astype(jnp.bfloat16)

    band_rows = lax.map(legendre_slot, (legendre, masked))
    fields_here = coeffs.shape[1] // 2

    def lat_synth(operands):
        lat_row, lon_total = operands
        twiddle = fourier_table(wave_of_slot, lon_total, 0, NLONMAX).astype(jnp.float32)
        paired = lat_row.reshape(M, fields_here, 2).astype(jnp.float32)
        result = jnp.einsum('sfc,csi->fi', paired, twiddle)
        return result.astype(jnp.bfloat16)

    grid_rows = lax.map(lat_synth, (jnp.transpose(band_rows, (1, 0, 2)), lon_count))
    return jnp.transpose(grid_rows, (1, 0, 2))
```

```python
import functools

import jax
import jax.numpy as jnp
from jax import lax
from jax.experimental import pallas as pl
from jax.experimental.pallas import tpu as pltpu
from jax.sharding import PartitionSpec as P

MESH = pl.DeviceIdType.MESH
LANES = 128
ROWS = 8
HALF = 256
COS_POLY = (1.0, -4.934802055358887, 4.058712005615234, -1.335260272026062, 0.23532071709632874,
            -0.025785624980926514, 0.001904185046441853, -8.864672417985275e-05)
SIN_POLY = (3.1415927410125732, -5.167712688446045, 2.5501604080200195, -0.5992420315742493,
            0.08208133280277252, -0.00727477390319109, 0.0003950836544390768)


def horner(poly, square):
    total = jnp.full_like(square, poly[-1])
    for value in poly[-2::-1]:
        total = total * square + value
    return total


def cos_sin(product, total, inverse):
    turns = jnp.round(product * (0.5 * inverse))
    part = (product - turns * (2.0 * total)) * inverse
    square = part * part
    return horner(COS_POLY, square), part * horner(SIN_POLY, square)


def iota(shape, dim):
    return lax.broadcasted_iota(jnp.int32, shape, dim)


def kernel(waves, groups, slots, fields,
           coef_hbm, leg_hbm, wave_smem, count_smem, wave_row, out_ref,
           coef, leg, packed, send_buf, recv_buf, arrived, spectra, wave_of_lane,
           fine_cos, fine_sin, coarse_cos, coarse_sin, mid_cos, mid_sin,
           table_cos, table_sin, real_part, imag_part, tile_buf,
           coef_sem, leg_sem, wave_send, wave_recv, lev_send, lev_recv):
    me = lax.axis_index("wave")
    group = lax.axis_index("lev")
    parts = 2 * fields
    degrees = coef.shape[2]
    kblocks = slots // 2
    width = out_ref.shape[2]

    def fetch(s):
        return (pltpu.make_async_copy(coef_hbm.at[s], coef.at[s], coef_sem.at[s]),
                pltpu.make_async_copy(leg_hbm.at[s], leg.at[s], leg_sem.at[s]))

    order = []
    for r in range(ROWS):
        order += [r, ROWS + r] + ([2 * ROWS + r] if r < slots - 2 * ROWS else [])
    for s in order:
        for copy in fetch(s):
            copy.start()

    barrier = pltpu.get_barrier_semaphore()

    @pl.loop(1, waves)
    def _(j):
        pl.semaphore_signal(barrier, inc=1, device_id=(lax.rem(me + j, waves), group), device_id_type=MESH)

    for j in range(1, groups):
        pl.semaphore_signal(barrier, inc=1, device_id=(me, lax.rem(group + j, groups)), device_id_type=MESH)

    degree = iota((1, degrees), 1)
    rest = slots - 2 * ROWS

    def legendre(s):
        for copy in fetch(s):
            copy.wait()
        limit = waves * slots - wave_smem[me * slots + s]
        mask = jnp.where(degree < limit, 1.0, 0.0).astype(jnp.bfloat16)
        return lax.dot_general(leg[s], coef[s] * mask, (((1,), (1,)), ((), ())),
                               preferred_element_type=jnp.float32)

    third = {}
    for r in range(ROWS):
        first = legendre(r)
        second = legendre(ROWS + r)
        if r < rest:
            third[r] = legendre(2 * ROWS + r)
            tail = third[r][:, :32]
        else:
            tail = jnp.concatenate([third[r - rest][:, 32:], jnp.zeros((waves, 16), jnp.float32)], axis=1)
        packed[pl.ds(r, waves, stride=ROWS), :] = jnp.concatenate([first, second, tail], axis=1)
    send_buf[...] = packed[...].reshape(waves, ROWS, LANES).astype(jnp.bfloat16)
    recv_buf[me] = send_buf[me]

    pl.semaphore_wait(barrier, waves + groups - 2)

    @pl.loop(1, waves)
    def _(j):
        target = lax.rem(me + j, waves)
        pltpu.make_async_remote_copy(
            src_ref=send_buf.at[target], dst_ref=recv_buf.at[me], send_sem=wave_send, recv_sem=wave_recv,
            device_id=(target, group), device_id_type=MESH).start()

    numbers = wave_row[...].astype(jnp.float32)
    high = jnp.floor(numbers * 0.125)
    low = numbers - 8.0 * high
    total_slots = waves * slots
    slot_row = iota((16, total_slots), 1)
    slot_in = lax.rem(slot_row, slots)
    block_of = iota((16, total_slots), 0)
    picked = []
    for value in (high, low):
        for parity in (0, 1):
            picked.append(jnp.where(slot_in == 2 * block_of + parity, value, 0.0))
    source = iota((2 * waves, total_slots), 1) // slots
    spread = jnp.where(source == lax.rem(iota((2 * waves, total_slots), 0), waves), 1.0, 0.0)
    gathered = lax.dot_general(jnp.concatenate(picked, axis=0).astype(jnp.bfloat16), spread.astype(jnp.bfloat16),
                               (((1,), (1,)), ((), ())), preferred_element_type=jnp.float32)
    even = 8.0 * gathered[0:16] + gathered[32:48]
    odd = 8.0 * gathered[16:32] + gathered[48:64]
    wave_of_lane[...] = jnp.where(iota((16, LANES), 1) < waves, even, odd)

    count = count_smem[0].astype(jnp.float32)
    total = jnp.full((1, LANES), count, jnp.float32)
    inverse = 1.0 / total
    row16 = iota((16, LANES), 0)
    fine_step = (2 * row16 + 1).astype(jnp.float32)
    coarse_step = (32 * row16).astype(jnp.float32)
    tile_at = (row16 >= 3).astype(jnp.int32) + (row16 >= 6).astype(jnp.int32) + (row16 >= 9).astype(jnp.int32)
    centre = row16 - 3 * tile_at
    tile_of = lax.rem(group + 1 + tile_at, groups)
    mid_step = (2 * width * tile_of + jnp.where(centre == 0, HALF * 2 - 1, jnp.where(centre == 1, HALF * 6 - 1, HALF * 8 - 1)))
    mid_step = mid_step.astype(jnp.float32)

    def tables(kb):
        lanes = pl.ds(kb * LANES, LANES)
        m = jnp.broadcast_to(wave_of_lane[pl.ds(kb, 1), :], (16, LANES))
        fc, fs = cos_sin(m * fine_step, total, inverse)
        fine_cos[:, lanes] = fc
        fine_sin[:, lanes] = fs
        cc, cs = cos_sin(m * coarse_step, total, inverse)
        coarse_cos[:, lanes] = cc
        coarse_sin[:, lanes] = cs
        mc, ms = cos_sin(m * mid_step, total, inverse)
        factor = jnp.where(2.0 * m <= total - 1.0, jnp.where(m == 0.0, 1.0, 2.0), 0.0)
        mid_cos[:, lanes] = factor * mc
        mid_sin[:, lanes] = factor * ms
        for a in range(HALF // 16):
            ca = coarse_cos[pl.ds(a, 1), lanes]
            sa = coarse_sin[pl.ds(a, 1), lanes]
            table_cos[pl.ds(16 * a, 16), lanes] = (ca * fc - sa * fs).astype(jnp.bfloat16)
            table_sin[pl.ds(16 * a, 16), lanes] = (sa * fc + ca * fs).astype(jnp.bfloat16)

    for kb in range(kblocks):
        tables(kb)
    flip = jnp.where(iota((HALF, HALF), 0) + iota((HALF, HALF), 1) == HALF - 1, 1.0, 0.0).astype(jnp.bfloat16)

    bulk = pltpu.make_async_remote_copy(
        src_ref=send_buf.at[pl.ds(0, waves - 1)], dst_ref=recv_buf.at[pl.ds(0, waves - 1)],
        send_sem=wave_send, recv_sem=wave_recv, device_id=(me, group), device_id_type=MESH)
    bulk.wait_recv()

    arrived[...] = recv_buf[...].astype(jnp.float32).reshape(waves * ROWS, LANES)
    for j in range(ROWS // 2):
        rows = jnp.concatenate([arrived[pl.ds(2 * j, waves, stride=ROWS), :],
                                arrived[pl.ds(2 * j + 1, waves, stride=ROWS), :]], axis=0)
        turned = rows.T
        spectra[pl.ds(j * parts, parts), :] = turned[0:parts]
        spectra[pl.ds((ROWS // 2 + j) * parts, parts), :] = turned[parts:2 * parts]
        if j < rest // 2:
            spectra[pl.ds((ROWS + j) * parts, 32), :] = turned[96:128]
        else:
            spectra[pl.ds((ROWS + j - rest // 2) * parts + 32, 16), :] = turned[96:112]

    for kb in range(kblocks):
        lanes = pl.ds(kb * LANES, LANES)
        re = spectra[pl.ds(kb * parts, fields, stride=2), :]
        im = spectra[pl.ds(kb * parts + 1, fields, stride=2), :]
        for pair in range(3 * groups // 2):
            real, imag = [], []
            for at in (2 * pair, 2 * pair + 1):
                c = mid_cos[pl.ds(at, 1), lanes]
                s = mid_sin[pl.ds(at, 1), lanes]
                real.append(re * c - im * s)
                imag.append(re * s + im * c)
            rows = pl.ds(pair * parts, parts)
            real_part[rows, lanes] = jnp.concatenate(real, axis=0).astype(jnp.bfloat16)
            imag_part[rows, lanes] = jnp.concatenate(imag, axis=0).astype(jnp.bfloat16)

    dims = (((1,), (1,)), ((), ()))
    even_sum = lax.dot_general(real_part[...], table_cos[...], dims, preferred_element_type=jnp.float32)
    odd_sum = lax.dot_general(imag_part[...], table_sin[...], dims, preferred_element_type=jnp.float32)
    ahead = even_sum - odd_sum
    behind = jnp.dot((even_sum + odd_sum).astype(jnp.bfloat16), flip, preferred_element_type=jnp.float32)
    lane = iota((1, HALF), 1)
    limit = count_smem[0]

    def piece(tile, base, at, values):
        values = values[fields * (3 * tile + at):fields * (3 * tile + at + 1)]
        start = width * lax.rem(group + 1 + tile, groups) + base
        return jnp.where(lane + start < limit, values, 0.0).astype(jnp.bfloat16)

    sends = []
    for tile in range(groups):
        pieces = [piece(tile, 0, 0, behind), piece(tile, HALF, 0, ahead), piece(tile, 2 * HALF, 1, behind),
                  piece(tile, 3 * HALF, 1, ahead), piece(tile, 4 * HALF, 2, ahead)]
        result = jnp.concatenate(pieces, axis=1)
        if tile < groups - 1:
            tile_buf[tile] = result
            copy = pltpu.make_async_remote_copy(
                src_ref=tile_buf.at[tile], dst_ref=out_ref.at[group], send_sem=lev_send.at[tile],
                recv_sem=lev_recv.at[tile], device_id=(me, lax.rem(group + 1 + tile, groups)), device_id_type=MESH)
            copy.start()
            sends.append(copy)
        else:
            out_ref[group] = result
    bulk.wait_send()
    for tile, copy in enumerate(sends):
        copy.wait_send()
        sender = lax.rem(group + groups - 1 - tile, groups)
        pltpu.make_async_remote_copy(
            src_ref=tile_buf.at[tile], dst_ref=out_ref.at[sender], send_sem=lev_send.at[tile],
            recv_sem=lev_recv.at[tile], device_id=(me, sender), device_id_type=MESH).wait_recv()


def solution(mesh):
    waves, groups = mesh.shape["wave"], mesh.shape["lev"]

    def per_device(coeffs, legendre, wave_of_slot, lon_count):
        slots, parts, degrees = coeffs.shape
        lats = legendre.shape[1]
        fields = parts // 2
        width = 5120 // groups
        total = waves * slots
        centres = 3 * groups
        f32, bf16 = jnp.float32, jnp.bfloat16
        vmem = pl.BlockSpec(memory_space=pltpu.VMEM)
        smem = pl.BlockSpec(memory_space=pltpu.SMEM)
        hbm = pl.BlockSpec(memory_space=pl.ANY)
        dma = pltpu.SemaphoreType.DMA
        out = pl.pallas_call(
            functools.partial(kernel, waves, groups, slots, fields),
            out_shape=jax.ShapeDtypeStruct((groups, fields, width), bf16),
            in_specs=[hbm, hbm, smem, smem, vmem],
            out_specs=vmem,
            scratch_shapes=[
                pltpu.VMEM((slots, parts, degrees), bf16),
                pltpu.VMEM((slots, lats, degrees), bf16),
                pltpu.VMEM((waves * ROWS, LANES), f32),
                pltpu.VMEM((waves, ROWS, LANES), bf16),
                pltpu.VMEM((waves, ROWS, LANES), bf16),
                pltpu.VMEM((waves * ROWS, LANES), f32),
                pltpu.VMEM((slots // 2 * parts, LANES), f32),
                pltpu.VMEM((16, LANES), f32),
                pltpu.VMEM((16, total), f32), pltpu.VMEM((16, total), f32),
                pltpu.VMEM((16, total), f32), pltpu.VMEM((16, total), f32),
                pltpu.VMEM((16, total), f32), pltpu.VMEM((16, total), f32),
                pltpu.VMEM((HALF, total), bf16), pltpu.VMEM((HALF, total), bf16),
                pltpu.VMEM((centres * fields, total), bf16), pltpu.VMEM((centres * fields, total), bf16),
                pltpu.VMEM((groups - 1, fields, width), bf16),
                dma((slots,)), dma((slots,)), dma, dma, dma((groups - 1,)), dma((groups - 1,)),
            ],
            compiler_params=pltpu.CompilerParams(
                collective_id=0, has_side_effects=True, vmem_limit_bytes=40 * 2 ** 20),
        )(coeffs, legendre, wave_of_slot, lon_count, wave_of_slot.reshape(1, total))
        return out.reshape(groups * fields, 1, width)

    return jax.shard_map(
        per_device,
        mesh=mesh,
        in_specs=(P("wave", "lev", None), P("wave", None, None), P(), P("wave")),
        out_specs=P(None, "wave", "lev"),
        check_vma=False,
    )
```

```python
import functools

import jax
import jax.numpy as jnp
from jax import lax
from jax.experimental import pallas as pl
from jax.experimental.pallas import tpu as pltpu
from jax.sharding import PartitionSpec as P

MESH = pl.DeviceIdType.MESH
LANES = 128
ROWS = 8
HALF = 256
GROUP = 2
COS_POLY = (1.0, -4.934802055358887, 4.058712005615234, -1.335260272026062, 0.23532071709632874,
            -0.025785624980926514, 0.001904185046441853, -8.864672417985275e-05)
SIN_POLY = (3.1415927410125732, -5.167712688446045, 2.5501604080200195, -0.5992420315742493,
            0.08208133280277252, -0.00727477390319109, 0.0003950836544390768)


def peers(me):
    steps = [(dz, dx, dc) for dz in range(8) for dx in range(4) for dc in range(2)][1:]
    steps.sort(key=lambda d: -(2 * min(d[0], 8 - d[0]) + 2 * min(d[1], 4 - d[1]) + d[2]))
    z, x, core = me // 8, lax.rem(me // 2, 4), lax.rem(me, 2)
    return [8 * lax.rem(z + dz, 8) + 2 * lax.rem(x + dx, 4) + (1 - core if dc else core) for dz, dx, dc in steps]


def horner(poly, square):
    total = jnp.full_like(square, poly[-1])
    for value in poly[-2::-1]:
        total = total * square + value
    return total


def cos_sin(product, total, inverse):
    turns = jnp.round(product * (0.5 * inverse))
    part = (product - turns * (2.0 * total)) * inverse
    square = part * part
    return horner(COS_POLY, square), part * horner(SIN_POLY, square)


def iota(shape, dim):
    return lax.broadcasted_iota(jnp.int32, shape, dim)


def kernel(waves, groups, slots, fields,
           coef_hbm, leg_hbm, wave_hbm, count_smem, out_ref,
           wave_smem, wave_rows, coef, leg, packed, send_buf, recv_buf, arrived, spectra, wave_of_lane,
           fine_cos, fine_sin, coarse_cos, coarse_sin, mid_cos, mid_sin,
           table_cos, table_sin, real_part, imag_part, tile_buf,
           wave_sem, coef_sem, leg_sem, wave_send, wave_recv, lev_send, lev_recv):
    me = lax.axis_index("wave")
    group = lax.axis_index("lev")
    parts = 2 * fields
    degrees = coef.shape[2]
    kblocks = slots // 2
    width = out_ref.shape[2]

    rest = slots - 2 * ROWS

    def fetch(g):
        starts = [2 * g, ROWS + 2 * g] + ([2 * ROWS + 2 * g] if 2 * g < rest else [])
        for n, at in enumerate(starts):
            two = pl.ds(at, 2)
            yield pltpu.make_async_copy(coef_hbm.at[two], coef.at[two], coef_sem.at[g, n])
            yield pltpu.make_async_copy(leg_hbm.at[two], leg.at[two], leg_sem.at[g, n])

    to_smem = pltpu.make_async_copy(wave_hbm, wave_smem, wave_sem.at[0])
    to_vmem = pltpu.make_async_copy(wave_hbm, wave_rows, wave_sem.at[1])
    to_smem.start()
    to_vmem.start()
    for g in range(ROWS // 2):
        for copy in fetch(g):
            copy.start()

    barrier = pltpu.get_barrier_semaphore()

    for target in peers(me):
        pl.semaphore_signal(barrier, inc=1, device_id=(target, group), device_id_type=MESH)

    for j in range(1, groups):
        pl.semaphore_signal(barrier, inc=1, device_id=(me, lax.rem(group + j, groups)), device_id_type=MESH)

    to_smem.wait()
    to_vmem.wait()

    degree = iota((1, degrees), 1)
    def number_of_slot(s):
        place = me * slots + s
        return wave_smem[place // LANES, lax.rem(place, LANES)]

    def legendre(s):
        limit = waves * slots - number_of_slot(s)
        mask = jnp.where(degree < limit, 1.0, 0.0).astype(jnp.bfloat16)
        return lax.dot_general(leg[s], coef[s] * mask, (((1,), (1,)), ((), ())),
                               preferred_element_type=jnp.float32)

    third = {}
    for r in range(ROWS):
        if r % GROUP == 0:
            for g in range(r // 2, (r + GROUP) // 2):
                for copy in fetch(g):
                    copy.wait()
        first = legendre(r)
        second = legendre(ROWS + r)
        if r < rest:
            third[r] = legendre(2 * ROWS + r)
            tail = third[r][:, :32]
        else:
            tail = jnp.concatenate([third[r - rest][:, 32:], jnp.zeros((waves, 16), jnp.float32)], axis=1)
        packed[pl.ds(r, waves, stride=ROWS), :] = jnp.concatenate([first, second, tail], axis=1)
    send_buf[...] = packed[...].reshape(waves, ROWS, LANES).astype(jnp.bfloat16)
    recv_buf[me] = send_buf[me]

    pl.semaphore_wait(barrier, waves + groups - 2)


    for target in peers(me):
        pltpu.make_async_remote_copy(
            src_ref=send_buf.at[target], dst_ref=recv_buf.at[me], send_sem=wave_send, recv_sem=wave_recv,
            device_id=(target, group), device_id_type=MESH).start()

    numbers = wave_rows[...].astype(jnp.float32)
    high = jnp.floor(numbers * 0.125)
    low = numbers - 8.0 * high
    block_of = iota((16, LANES), 0)
    lane_of = iota((2 * waves, LANES), 0)
    gathered = jnp.zeros((64, 2 * waves), jnp.float32)
    for row in range(kblocks):
        slot_of = iota((1, LANES), 1) + row * LANES
        source = slot_of // slots
        slot_in = slot_of - slots * source
        picked = [jnp.where(slot_in == 2 * block_of + parity, value[row:row + 1], 0.0)
                  for value in (high, low) for parity in (0, 1)]
        spread = jnp.where((source == lane_of) | (source + waves == lane_of), 1.0, 0.0)
        gathered += lax.dot_general(jnp.concatenate(picked, axis=0).astype(jnp.bfloat16), spread.astype(jnp.bfloat16),
                                    (((1,), (1,)), ((), ())), preferred_element_type=jnp.float32)
    even = 8.0 * gathered[0:16] + gathered[32:48]
    odd = 8.0 * gathered[16:32] + gathered[48:64]
    wave_of_lane[...] = jnp.where(iota((16, LANES), 1) < waves, even, odd)

    count = count_smem[0].astype(jnp.float32)
    total = jnp.full((1, LANES), count, jnp.float32)
    inverse = 1.0 / total
    row16 = iota((16, LANES), 0)
    fine_step = (2 * row16 + 1).astype(jnp.float32)
    coarse_step = (32 * row16).astype(jnp.float32)
    tile_at = (row16 >= 3).astype(jnp.int32) + (row16 >= 6).astype(jnp.int32) + (row16 >= 9).astype(jnp.int32)
    centre = row16 - 3 * tile_at
    tile_of = lax.rem(group + 1 + tile_at, groups)
    mid_step = (2 * width * tile_of + jnp.where(centre == 0, HALF * 2 - 1, jnp.where(centre == 1, HALF * 6 - 1, HALF * 8 - 1)))
    mid_step = mid_step.astype(jnp.float32)

    def tables(kb):
        lanes = pl.ds(kb * LANES, LANES)
        m = jnp.broadcast_to(wave_of_lane[pl.ds(kb, 1), :], (16, LANES))
        fc, fs = cos_sin(m * fine_step, total, inverse)
        fine_cos[:, lanes] = fc
        fine_sin[:, lanes] = fs
        cc, cs = cos_sin(m * coarse_step, total, inverse)
        coarse_cos[:, lanes] = cc
        coarse_sin[:, lanes] = cs
        mc, ms = cos_sin(m * mid_step, total, inverse)
        factor = jnp.where(2.0 * m <= total - 1.0, jnp.where(m == 0.0, 1.0, 2.0), 0.0)
        mid_cos[:, lanes] = factor * mc
        mid_sin[:, lanes] = factor * ms
        for a in range(HALF // 16):
            ca = coarse_cos[pl.ds(a, 1), lanes]
            sa = coarse_sin[pl.ds(a, 1), lanes]
            table_cos[pl.ds(16 * a, 16), lanes] = (ca * fc - sa * fs).astype(jnp.bfloat16)
            table_sin[pl.ds(16 * a, 16), lanes] = (sa * fc + ca * fs).astype(jnp.bfloat16)

    for kb in range(kblocks):
        tables(kb)
    flip = jnp.where(iota((HALF, HALF), 0) + iota((HALF, HALF), 1) == HALF - 1, 1.0, 0.0).astype(jnp.bfloat16)

    bulk = pltpu.make_async_remote_copy(
        src_ref=send_buf.at[pl.ds(0, waves - 1)], dst_ref=recv_buf.at[pl.ds(0, waves - 1)],
        send_sem=wave_send, recv_sem=wave_recv, device_id=(me, group), device_id_type=MESH)
    bulk.wait_recv()

    arrived[...] = recv_buf[...].astype(jnp.float32).reshape(waves * ROWS, LANES)
    for j in range(ROWS // 2):
        rows = jnp.concatenate([arrived[pl.ds(2 * j, waves, stride=ROWS), :],
                                arrived[pl.ds(2 * j + 1, waves, stride=ROWS), :]], axis=0)
        turned = rows.T
        spectra[pl.ds(j * parts, parts), :] = turned[0:parts]
        spectra[pl.ds((ROWS // 2 + j) * parts, parts), :] = turned[parts:2 * parts]
        if j < rest // 2:
            spectra[pl.ds((ROWS + j) * parts, 32), :] = turned[96:128]
        else:
            spectra[pl.ds((ROWS + j - rest // 2) * parts + 32, 16), :] = turned[96:112]

    for kb in range(kblocks):
        lanes = pl.ds(kb * LANES, LANES)
        re = spectra[pl.ds(kb * parts, fields, stride=2), :]
        im = spectra[pl.ds(kb * parts + 1, fields, stride=2), :]
        for pair in range(3 * groups // 2):
            real, imag = [], []
            for at in (2 * pair, 2 * pair + 1):
                c = mid_cos[pl.ds(at, 1), lanes]
                s = mid_sin[pl.ds(at, 1), lanes]
                real.append(re * c - im * s)
                imag.append(re * s + im * c)
            rows = pl.ds(pair * parts, parts)
            real_part[rows, lanes] = jnp.concatenate(real, axis=0).astype(jnp.bfloat16)
            imag_part[rows, lanes] = jnp.concatenate(imag, axis=0).astype(jnp.bfloat16)

    dims = (((1,), (1,)), ((), ()))
    even_sum = lax.dot_general(real_part[...], table_cos[...], dims, preferred_element_type=jnp.float32)
    odd_sum = lax.dot_general(imag_part[...], table_sin[...], dims, preferred_element_type=jnp.float32)
    ahead = even_sum - odd_sum
    behind = jnp.dot((even_sum + odd_sum).astype(jnp.bfloat16), flip, preferred_element_type=jnp.float32)
    lane = iota((1, HALF), 1)
    limit = count_smem[0]

    def piece(tile, base, at, values):
        values = values[fields * (3 * tile + at):fields * (3 * tile + at + 1)]
        start = width * lax.rem(group + 1 + tile, groups) + base
        return jnp.where(lane + start < limit, values, 0.0).astype(jnp.bfloat16)

    sends = []
    for tile in range(groups):
        pieces = [piece(tile, 0, 0, behind), piece(tile, HALF, 0, ahead), piece(tile, 2 * HALF, 1, behind),
                  piece(tile, 3 * HALF, 1, ahead), piece(tile, 4 * HALF, 2, ahead)]
        result = jnp.concatenate(pieces, axis=1)
        if tile < groups - 1:
            tile_buf[tile] = result
            copy = pltpu.make_async_remote_copy(
                src_ref=tile_buf.at[tile], dst_ref=out_ref.at[group], send_sem=lev_send.at[tile],
                recv_sem=lev_recv.at[tile], device_id=(me, lax.rem(group + 1 + tile, groups)), device_id_type=MESH)
            copy.start()
            sends.append(copy)
        else:
            out_ref[group] = result
    bulk.wait_send()
    for tile, copy in enumerate(sends):
        copy.wait_send()
        sender = lax.rem(group + groups - 1 - tile, groups)
        pltpu.make_async_remote_copy(
            src_ref=tile_buf.at[tile], dst_ref=out_ref.at[sender], send_sem=lev_send.at[tile],
            recv_sem=lev_recv.at[tile], device_id=(me, sender), device_id_type=MESH).wait_recv()


def solution(mesh):
    waves, groups = mesh.shape["wave"], mesh.shape["lev"]

    def per_device(coeffs, legendre, wave_of_slot, lon_count):
        slots, parts, degrees = coeffs.shape
        lats = legendre.shape[1]
        fields = parts // 2
        width = 5120 // groups
        total = waves * slots
        centres = 3 * groups
        f32, bf16 = jnp.float32, jnp.bfloat16
        vmem = pl.BlockSpec(memory_space=pltpu.VMEM)
        smem = pl.BlockSpec(memory_space=pltpu.SMEM)
        hbm = pl.BlockSpec(memory_space=pltpu.HBM)
        dma = pltpu.SemaphoreType.DMA
        out = pl.pallas_call(
            functools.partial(kernel, waves, groups, slots, fields),
            out_shape=jax.ShapeDtypeStruct((groups, fields, width), bf16),
            in_specs=[hbm, hbm, hbm, smem],
            out_specs=vmem,
            scratch_shapes=[
                pltpu.SMEM((total // LANES, LANES), jnp.int32),
                pltpu.VMEM((total // LANES, LANES), jnp.int32),
                pltpu.VMEM((slots, parts, degrees), bf16),
                pltpu.VMEM((slots, lats, degrees), bf16),
                pltpu.VMEM((waves * ROWS, LANES), f32),
                pltpu.VMEM((waves, ROWS, LANES), bf16),
                pltpu.VMEM((waves, ROWS, LANES), bf16),
                pltpu.VMEM((waves * ROWS, LANES), f32),
                pltpu.VMEM((slots // 2 * parts, LANES), f32),
                pltpu.VMEM((16, LANES), f32),
                pltpu.VMEM((16, total), f32), pltpu.VMEM((16, total), f32),
                pltpu.VMEM((16, total), f32), pltpu.VMEM((16, total), f32),
                pltpu.VMEM((16, total), f32), pltpu.VMEM((16, total), f32),
                pltpu.VMEM((HALF, total), bf16), pltpu.VMEM((HALF, total), bf16),
                pltpu.VMEM((centres * fields, total), bf16), pltpu.VMEM((centres * fields, total), bf16),
                pltpu.VMEM((groups - 1, fields, width), bf16),
                dma((2,)), dma((ROWS // 2, 3)), dma((ROWS // 2, 3)), dma, dma, dma((groups - 1,)), dma((groups - 1,)),
            ],
            compiler_params=pltpu.CompilerParams(
                collective_id=0, has_side_effects=True,
 vmem_limit_bytes=53 * 2 ** 20),
        )(coeffs, legendre, pltpu.with_memory_space_constraint(wave_of_slot.reshape(total // LANES, LANES), pltpu.HBM), lon_count)
        return out.reshape(groups * fields, 1, width)

    return jax.shard_map(
        per_device,
        mesh=mesh,
        in_specs=(P("wave", "lev", None), P("wave", None, None), P(), P("wave")),
        out_specs=P(None, "wave", "lev"),
        check_vma=False,
    )
```

```python
import functools

import jax
import jax.numpy as jnp
from jax import lax
from jax.experimental import pallas as pl
from jax.experimental.pallas import tpu as pltpu
from jax.sharding import PartitionSpec as P

MESH = pl.DeviceIdType.MESH
LANES = 128
ROWS = 8
HALF = 256
GROUP = 2
COS_POLY = (1.0, -4.934802055358887, 4.058712005615234, -1.335260272026062, 0.23532071709632874,
            -0.025785624980926514, 0.001904185046441853, -8.864672417985275e-05)
SIN_POLY = (3.1415927410125732, -5.167712688446045, 2.5501604080200195, -0.5992420315742493,
            0.08208133280277252, -0.00727477390319109, 0.0003950836544390768)


LATE_Z = (0, 2, 4, 7, 14, 14, 14, 14)
LATE_X = (0, 3, 5, 3)
WAVE_ORDER = sorted(range(64), key=lambda w: (LATE_Z[w // 8] + LATE_X[w // 2 % 4], -(w % 2), w))


def horner(poly, square):
    total = jnp.full_like(square, poly[-1])
    for value in poly[-2::-1]:
        total = total * square + value
    return total


def cos_sin(product, total, inverse):
    turns = jnp.round(product * (0.5 * inverse))
    part = (product - turns * (2.0 * total)) * inverse
    square = part * part
    return horner(COS_POLY, square), part * horner(SIN_POLY, square)


def iota(shape, dim):
    return lax.broadcasted_iota(jnp.int32, shape, dim)


def kernel(waves, groups, slots, fields,
           coef_hbm, leg_hbm, wave_hbm, count_smem, out_ref,
           wave_smem, wave_rows, coef, leg, packed, send_buf, recv_buf, arrived, spectra, wave_of_lane,
           fine_cos, fine_sin, coarse_cos, coarse_sin, mid_cos, mid_sin,
           table_cos, table_sin, real_part, imag_part, tile_buf,
           wave_sem, coef_sem, leg_sem, wave_send, wave_recv, lev_send, lev_recv):
    me = lax.axis_index("wave")
    group = lax.axis_index("lev")
    parts = 2 * fields
    degrees = coef.shape[2]
    kblocks = slots // 2
    width = out_ref.shape[2]

    rest = slots - 2 * ROWS

    def fetch(g):
        starts = [2 * g, ROWS + 2 * g] + ([2 * ROWS + 2 * g] if 2 * g < rest else [])
        for n, at in enumerate(starts):
            two = pl.ds(at, 2)
            yield pltpu.make_async_copy(coef_hbm.at[two], coef.at[two], coef_sem.at[g, n])
            yield pltpu.make_async_copy(leg_hbm.at[two], leg.at[two], leg_sem.at[g, n])

    to_smem = pltpu.make_async_copy(wave_hbm, wave_smem, wave_sem.at[0])
    to_vmem = pltpu.make_async_copy(wave_hbm, wave_rows, wave_sem.at[1])
    to_smem.start()
    to_vmem.start()
    for g in range(ROWS // 2):
        for copy in fetch(g):
            copy.start()

    barrier = pltpu.get_barrier_semaphore()

    for target in WAVE_ORDER:
        @pl.when(me != target)
        def _():
            pl.semaphore_signal(barrier, inc=1, device_id=(target, group), device_id_type=MESH)

    for j in range(1, groups):
        pl.semaphore_signal(barrier, inc=1, device_id=(me, lax.rem(group + j, groups)), device_id_type=MESH)

    to_smem.wait()
    to_vmem.wait()

    degree = iota((1, degrees), 1)
    def number_of_slot(s):
        place = me * slots + s
        return wave_smem[place // LANES, lax.rem(place, LANES)]

    def legendre(s):
        limit = waves * slots - number_of_slot(s)
        mask = jnp.where(degree < limit, 1.0, 0.0).astype(jnp.bfloat16)
        return lax.dot_general(leg[s], coef[s] * mask, (((1,), (1,)), ((), ())),
                               preferred_element_type=jnp.float32)

    third = {}
    for r in range(ROWS):
        if r % GROUP == 0:
            for g in range(r // 2, (r + GROUP) // 2):
                for copy in fetch(g):
                    copy.wait()
        first = legendre(r)
        second = legendre(ROWS + r)
        if r < rest:
            third[r] = legendre(2 * ROWS + r)
            tail = third[r][:, :32]
        else:
            tail = jnp.concatenate([third[r - rest][:, 32:], jnp.zeros((waves, 16), jnp.float32)], axis=1)
        packed[pl.ds(r, waves, stride=ROWS), :] = jnp.concatenate([first, second, tail], axis=1)
    send_buf[...] = packed[...].reshape(waves, ROWS, LANES).astype(jnp.bfloat16)
    recv_buf[me] = send_buf[me]

    pl.semaphore_wait(barrier, waves + groups - 2)


    for target in WAVE_ORDER:
        @pl.when(me != target)
        def _():
            pltpu.make_async_remote_copy(
                src_ref=send_buf.at[target], dst_ref=recv_buf.at[me], send_sem=wave_send, recv_sem=wave_recv,
                device_id=(target, group), device_id_type=MESH).start()

    numbers = wave_rows[...].astype(jnp.float32)
    high = jnp.floor(numbers * 0.125)
    low = numbers - 8.0 * high
    block_of = iota((16, LANES), 0)
    lane_of = iota((2 * waves, LANES), 0)
    gathered = jnp.zeros((64, 2 * waves), jnp.float32)
    for row in range(kblocks):
        slot_of = iota((1, LANES), 1) + row * LANES
        source = slot_of // slots
        slot_in = slot_of - slots * source
        picked = [jnp.where(slot_in == 2 * block_of + parity, value[row:row + 1], 0.0)
                  for value in (high, low) for parity in (0, 1)]
        spread = jnp.where((source == lane_of) | (source + waves == lane_of), 1.0, 0.0)
        gathered += lax.dot_general(jnp.concatenate(picked, axis=0).astype(jnp.bfloat16), spread.astype(jnp.bfloat16),
                                    (((1,), (1,)), ((), ())), preferred_element_type=jnp.float32)
    even = 8.0 * gathered[0:16] + gathered[32:48]
    odd = 8.0 * gathered[16:32] + gathered[48:64]
    wave_of_lane[...] = jnp.where(iota((16, LANES), 1) < waves, even, odd)

    count = count_smem[0].astype(jnp.float32)
    total = jnp.full((1, LANES), count, jnp.float32)
    inverse = 1.0 / total
    row16 = iota((16, LANES), 0)
    fine_step = (2 * row16 + 1).astype(jnp.float32)
    coarse_step = (32 * row16).astype(jnp.float32)
    tile_at = (row16 >= 3).astype(jnp.int32) + (row16 >= 6).astype(jnp.int32) + (row16 >= 9).astype(jnp.int32)
    centre = row16 - 3 * tile_at
    tile_of = lax.rem(group + 1 + tile_at, groups)
    mid_step = (2 * width * tile_of + jnp.where(centre == 0, HALF * 2 - 1, jnp.where(centre == 1, HALF * 6 - 1, HALF * 8 - 1)))
    mid_step = mid_step.astype(jnp.float32)

    def tables(kb):
        lanes = pl.ds(pl.multiple_of(kb * LANES, LANES), LANES)
        m = jnp.broadcast_to(wave_of_lane[pl.ds(kb, 1), :], (16, LANES))
        fc, fs = cos_sin(m * fine_step, total, inverse)
        fine_cos[:, lanes] = fc
        fine_sin[:, lanes] = fs
        cc, cs = cos_sin(m * coarse_step, total, inverse)
        coarse_cos[:, lanes] = cc
        coarse_sin[:, lanes] = cs
        mc, ms = cos_sin(m * mid_step, total, inverse)
        factor = jnp.where(2.0 * m <= total - 1.0, jnp.where(m == 0.0, 1.0, 2.0), 0.0)
        mid_cos[:, lanes] = factor * mc
        mid_sin[:, lanes] = factor * ms
        for a in range(HALF // 16):
            ca = coarse_cos[pl.ds(a, 1), lanes]
            sa = coarse_sin[pl.ds(a, 1), lanes]
            table_cos[pl.ds(16 * a, 16), lanes] = (ca * fc - sa * fs).astype(jnp.bfloat16)
            table_sin[pl.ds(16 * a, 16), lanes] = (sa * fc + ca * fs).astype(jnp.bfloat16)

    pl.loop(0, kblocks)(tables)
    flip = jnp.where(iota((HALF, HALF), 0) + iota((HALF, HALF), 1) == HALF - 1, 1.0, 0.0).astype(jnp.bfloat16)

    bulk = pltpu.make_async_remote_copy(
        src_ref=send_buf.at[pl.ds(0, waves - 1)], dst_ref=recv_buf.at[pl.ds(0, waves - 1)],
        send_sem=wave_send, recv_sem=wave_recv, device_id=(me, group), device_id_type=MESH)
    bulk.wait_recv()

    arrived[...] = recv_buf[...].astype(jnp.float32).reshape(waves * ROWS, LANES)
    for j in range(ROWS // 2):
        rows = jnp.concatenate([arrived[pl.ds(2 * j, waves, stride=ROWS), :],
                                arrived[pl.ds(2 * j + 1, waves, stride=ROWS), :]], axis=0)
        turned = rows.T
        spectra[pl.ds(j * parts, parts), :] = turned[0:parts]
        spectra[pl.ds((ROWS // 2 + j) * parts, parts), :] = turned[parts:2 * parts]
        if j < rest // 2:
            spectra[pl.ds((ROWS + j) * parts, 32), :] = turned[96:128]
        else:
            spectra[pl.ds((ROWS + j - rest // 2) * parts + 32, 16), :] = turned[96:112]

    for kb in range(kblocks):
        lanes = pl.ds(kb * LANES, LANES)
        re = spectra[pl.ds(kb * parts, fields, stride=2), :]
        im = spectra[pl.ds(kb * parts + 1, fields, stride=2), :]
        for pair in range(3 * groups // 2):
            real, imag = [], []
            for at in (2 * pair, 2 * pair + 1):
                c = mid_cos[pl.ds(at, 1), lanes]
                s = mid_sin[pl.ds(at, 1), lanes]
                real.append(re * c - im * s)
                imag.append(re * s + im * c)
            rows = pl.ds(pair * parts, parts)
            real_part[rows, lanes] = jnp.concatenate(real, axis=0).astype(jnp.bfloat16)
            imag_part[rows, lanes] = jnp.concatenate(imag, axis=0).astype(jnp.bfloat16)

    dims = (((1,), (1,)), ((), ()))
    even_sum = lax.dot_general(real_part[...], table_cos[...], dims, preferred_element_type=jnp.float32)
    odd_sum = lax.dot_general(imag_part[...], table_sin[...], dims, preferred_element_type=jnp.float32)
    ahead = even_sum - odd_sum
    behind = jnp.dot((even_sum + odd_sum).astype(jnp.bfloat16), flip, preferred_element_type=jnp.float32)
    lane = iota((1, HALF), 1)
    limit = count_smem[0]

    def piece(tile, base, at, values):
        values = values[fields * (3 * tile + at):fields * (3 * tile + at + 1)]
        start = width * lax.rem(group + 1 + tile, groups) + base
        return jnp.where(lane + start < limit, values, 0.0).astype(jnp.bfloat16)

    sends = []
    for tile in range(groups):
        pieces = [piece(tile, 0, 0, behind), piece(tile, HALF, 0, ahead), piece(tile, 2 * HALF, 1, behind),
                  piece(tile, 3 * HALF, 1, ahead), piece(tile, 4 * HALF, 2, ahead)]
        result = jnp.concatenate(pieces, axis=1)
        if tile < groups - 1:
            tile_buf[tile] = result
            copy = pltpu.make_async_remote_copy(
                src_ref=tile_buf.at[tile], dst_ref=out_ref.at[group], send_sem=lev_send.at[tile],
                recv_sem=lev_recv.at[tile], device_id=(me, lax.rem(group + 1 + tile, groups)), device_id_type=MESH)
            copy.start()
            sends.append(copy)
        else:
            out_ref[group] = result
    bulk.wait_send()
    for tile, copy in enumerate(sends):
        copy.wait_send()
        sender = lax.rem(group + groups - 1 - tile, groups)
        pltpu.make_async_remote_copy(
            src_ref=tile_buf.at[tile], dst_ref=out_ref.at[sender], send_sem=lev_send.at[tile],
            recv_sem=lev_recv.at[tile], device_id=(me, sender), device_id_type=MESH).wait_recv()


def solution(mesh):
    waves, groups = mesh.shape["wave"], mesh.shape["lev"]

    def per_device(coeffs, legendre, wave_of_slot, lon_count):
        slots, parts, degrees = coeffs.shape
        lats = legendre.shape[1]
        fields = parts // 2
        width = 5120 // groups
        total = waves * slots
        centres = 3 * groups
        f32, bf16 = jnp.float32, jnp.bfloat16
        vmem = pl.BlockSpec(memory_space=pltpu.VMEM)
        smem = pl.BlockSpec(memory_space=pltpu.SMEM)
        hbm = pl.BlockSpec(memory_space=pltpu.HBM)
        dma = pltpu.SemaphoreType.DMA
        out = pl.pallas_call(
            functools.partial(kernel, waves, groups, slots, fields),
            out_shape=jax.ShapeDtypeStruct((groups, fields, width), bf16),
            in_specs=[hbm, hbm, hbm, smem],
            out_specs=vmem,
            scratch_shapes=[
                pltpu.SMEM((total // LANES, LANES), jnp.int32),
                pltpu.VMEM((total // LANES, LANES), jnp.int32),
                pltpu.VMEM((slots, parts, degrees), bf16),
                pltpu.VMEM((slots, lats, degrees), bf16),
                pltpu.VMEM((waves * ROWS, LANES), f32),
                pltpu.VMEM((waves, ROWS, LANES), bf16),
                pltpu.VMEM((waves, ROWS, LANES), bf16),
                pltpu.VMEM((waves * ROWS, LANES), f32),
                pltpu.VMEM((slots // 2 * parts, LANES), f32),
                pltpu.VMEM((16, LANES), f32),
                pltpu.VMEM((16, total), f32), pltpu.VMEM((16, total), f32),
                pltpu.VMEM((16, total), f32), pltpu.VMEM((16, total), f32),
                pltpu.VMEM((16, total), f32), pltpu.VMEM((16, total), f32),
                pltpu.VMEM((HALF, total), bf16), pltpu.VMEM((HALF, total), bf16),
                pltpu.VMEM((centres * fields, total), bf16), pltpu.VMEM((centres * fields, total), bf16),
                pltpu.VMEM((groups - 1, fields, width), bf16),
                dma((2,)), dma((ROWS // 2, 3)), dma((ROWS // 2, 3)), dma, dma, dma((groups - 1,)), dma((groups - 1,)),
            ],
            compiler_params=pltpu.CompilerParams(
                collective_id=0, has_side_effects=True,
 vmem_limit_bytes=53 * 2 ** 20),
        )(coeffs, legendre, pltpu.with_memory_space_constraint(wave_of_slot.reshape(total // LANES, LANES), pltpu.HBM), lon_count)
        return out.reshape(groups * fields, 1, width)

    return jax.shard_map(
        per_device,
        mesh=mesh,
        in_specs=(P("wave", "lev", None), P("wave", None, None), P(), P("wave")),
        out_specs=P(None, "wave", "lev"),
        check_vma=False,
    )
```

```python
import functools

import jax
import jax.numpy as jnp
from jax import lax
from jax.experimental import pallas as pl
from jax.experimental.pallas import tpu as pltpu
from jax.sharding import PartitionSpec as P

MESH = pl.DeviceIdType.MESH
LANES = 128
ROWS = 8
HALF = 256
STEPS = ((0, 4), (4, 4))
COS_POLY = (1.0, -4.934802055358887, 4.058712005615234, -1.335260272026062, 0.23532071709632874,
            -0.025785624980926514, 0.001904185046441853, -8.864672417985275e-05)
SIN_POLY = (3.1415927410125732, -5.167712688446045, 2.5501604080200195, -0.5992420315742493,
            0.08208133280277252, -0.00727477390319109, 0.0003950836544390768)


LATE_Z = (0, 2, 4, 7, 14, 14, 14, 14)
LATE_X = (0, 3, 5, 3)
WAVE_ORDER = sorted(range(64), key=lambda w: (LATE_Z[w // 8] + LATE_X[w // 2 % 4], -(w % 2), w))


def horner(poly, square):
    total = jnp.full_like(square, poly[-1])
    for value in poly[-2::-1]:
        total = total * square + value
    return total


def cos_sin(product, total, inverse):
    turns = jnp.round(product * (0.5 * inverse))
    part = (product - turns * (2.0 * total)) * inverse
    square = part * part
    return horner(COS_POLY, square), part * horner(SIN_POLY, square)


def iota(shape, dim):
    return lax.broadcasted_iota(jnp.int32, shape, dim)


def kernel(waves, groups, slots, fields,
           coef_hbm, leg_hbm, wave_hbm, count_hbm, out_ref,
           count_smem, wave_smem, wave_rows, coef, leg, packed, send_buf, recv_buf, arrived, spectra, wave_of_lane,
           fine_cos, fine_sin, coarse_cos, coarse_sin, mid_cos, mid_sin,
           table_cos, table_sin, real_part, imag_part, tile_buf,
           wave_sem, coef_sem, leg_sem, wave_send, wave_recv, lev_send, lev_recv):
    me = lax.axis_index("wave")
    group = lax.axis_index("lev")
    parts = 2 * fields
    degrees = coef.shape[2]
    kblocks = slots // 2
    width = out_ref.shape[2]

    rest = slots - 2 * ROWS

    def fetch(step):
        first, many = STEPS[step]
        starts = [first, ROWS + first] + ([2 * ROWS + first] if first < rest else [])
        for n, at in enumerate(starts):
            these = pl.ds(at, many)
            yield pltpu.make_async_copy(coef_hbm.at[these], coef.at[these], coef_sem.at[step, n])
            yield pltpu.make_async_copy(leg_hbm.at[these], leg.at[these], leg_sem.at[step, n])

    to_smem = pltpu.make_async_copy(wave_hbm, wave_smem, wave_sem.at[0])
    to_vmem = pltpu.make_async_copy(wave_hbm, wave_rows, wave_sem.at[1])
    to_count = pltpu.make_async_copy(count_hbm, count_smem, wave_sem.at[2])
    to_smem.start()
    to_vmem.start()
    to_count.start()
    for step in range(len(STEPS)):
        for copy in fetch(step):
            copy.start()

    barrier = pltpu.get_barrier_semaphore()

    for target in WAVE_ORDER:
        @pl.when(me != target)
        def _():
            pl.semaphore_signal(barrier, inc=1, device_id=(target, group), device_id_type=MESH)

    for j in range(1, groups):
        pl.semaphore_signal(barrier, inc=1, device_id=(me, lax.rem(group + j, groups)), device_id_type=MESH)

    to_smem.wait()
    to_vmem.wait()
    to_count.wait()

    degree = iota((1, degrees), 1)
    def number_of_slot(s):
        place = me * slots + s
        return wave_smem[place // LANES, lax.rem(place, LANES)]

    def legendre(s):
        limit = waves * slots - number_of_slot(s)
        mask = jnp.where(degree < limit, 1.0, 0.0).astype(jnp.bfloat16)
        return lax.dot_general(leg[s], coef[s] * mask, (((1,), (1,)), ((), ())),
                               preferred_element_type=jnp.float32)

    third = {}
    for r in range(ROWS):
        for step, (start, _) in enumerate(STEPS):
            if start == r:
                for copy in fetch(step):
                    copy.wait()
        first = legendre(r)
        second = legendre(ROWS + r)
        if r < rest:
            third[r] = legendre(2 * ROWS + r)
            tail = third[r][:, :32]
        else:
            tail = jnp.concatenate([third[r - rest][:, 32:], jnp.zeros((waves, 16), jnp.float32)], axis=1)
        packed[pl.ds(r, waves, stride=ROWS), :] = jnp.concatenate([first, second, tail], axis=1)
    send_buf[...] = packed[...].reshape(waves, ROWS, LANES).astype(jnp.bfloat16)
    recv_buf[me] = send_buf[me]

    pl.semaphore_wait(barrier, waves + groups - 2)


    for target in WAVE_ORDER:
        @pl.when(me != target)
        def _():
            pltpu.make_async_remote_copy(
                src_ref=send_buf.at[target], dst_ref=recv_buf.at[me], send_sem=wave_send, recv_sem=wave_recv,
                device_id=(target, group), device_id_type=MESH).start()

    numbers = wave_rows[...].astype(jnp.float32)
    high = jnp.floor(numbers * 0.125)
    low = numbers - 8.0 * high
    block_of = iota((16, LANES), 0)
    lane_of = iota((2 * waves, LANES), 0)
    gathered = jnp.zeros((64, 2 * waves), jnp.float32)
    for row in range(kblocks):
        slot_of = iota((1, LANES), 1) + row * LANES
        source = slot_of // slots
        slot_in = slot_of - slots * source
        picked = [jnp.where(slot_in == 2 * block_of + parity, value[row:row + 1], 0.0)
                  for value in (high, low) for parity in (0, 1)]
        spread = jnp.where((source == lane_of) | (source + waves == lane_of), 1.0, 0.0)
        gathered += lax.dot_general(jnp.concatenate(picked, axis=0).astype(jnp.bfloat16), spread.astype(jnp.bfloat16),
                                    (((1,), (1,)), ((), ())), preferred_element_type=jnp.float32)
    even = 8.0 * gathered[0:16] + gathered[32:48]
    odd = 8.0 * gathered[16:32] + gathered[48:64]
    wave_of_lane[...] = jnp.where(iota((16, LANES), 1) < waves, even, odd)

    count = count_smem[0, 0].astype(jnp.float32)
    total = jnp.full((1, LANES), count, jnp.float32)
    inverse = 1.0 / total
    row16 = iota((16, LANES), 0)
    fine_step = (2 * row16 + 1).astype(jnp.float32)
    coarse_step = (32 * row16).astype(jnp.float32)
    tile_at = (row16 >= 3).astype(jnp.int32) + (row16 >= 6).astype(jnp.int32) + (row16 >= 9).astype(jnp.int32)
    centre = row16 - 3 * tile_at
    tile_of = lax.rem(group + 1 + tile_at, groups)
    mid_step = (2 * width * tile_of + jnp.where(centre == 0, HALF * 2 - 1, jnp.where(centre == 1, HALF * 6 - 1, HALF * 8 - 1)))
    mid_step = mid_step.astype(jnp.float32)

    def tables(kb):
        lanes = pl.ds(pl.multiple_of(kb * LANES, LANES), LANES)
        m = jnp.broadcast_to(wave_of_lane[pl.ds(kb, 1), :], (16, LANES))
        fc, fs = cos_sin(m * fine_step, total, inverse)
        fine_cos[:, lanes] = fc
        fine_sin[:, lanes] = fs
        cc, cs = cos_sin(m * coarse_step, total, inverse)
        coarse_cos[:, lanes] = cc
        coarse_sin[:, lanes] = cs
        mc, ms = cos_sin(m * mid_step, total, inverse)
        factor = jnp.where(2.0 * m <= total - 1.0, jnp.where(m == 0.0, 1.0, 2.0), 0.0)
        mid_cos[:, lanes] = factor * mc
        mid_sin[:, lanes] = factor * ms
        for a in range(HALF // 16):
            ca = coarse_cos[pl.ds(a, 1), lanes]
            sa = coarse_sin[pl.ds(a, 1), lanes]
            table_cos[pl.ds(16 * a, 16), lanes] = (ca * fc - sa * fs).astype(jnp.bfloat16)
            table_sin[pl.ds(16 * a, 16), lanes] = (sa * fc + ca * fs).astype(jnp.bfloat16)

    pl.loop(0, kblocks)(tables)
    flip = jnp.where(iota((HALF, HALF), 0) + iota((HALF, HALF), 1) == HALF - 1, 1.0, 0.0).astype(jnp.bfloat16)

    bulk = pltpu.make_async_remote_copy(
        src_ref=send_buf.at[pl.ds(0, waves - 1)], dst_ref=recv_buf.at[pl.ds(0, waves - 1)],
        send_sem=wave_send, recv_sem=wave_recv, device_id=(me, group), device_id_type=MESH)
    bulk.wait_recv()

    arrived[...] = recv_buf[...].astype(jnp.float32).reshape(waves * ROWS, LANES)
    for j in range(ROWS // 2):
        rows = jnp.concatenate([arrived[pl.ds(2 * j, waves, stride=ROWS), :],
                                arrived[pl.ds(2 * j + 1, waves, stride=ROWS), :]], axis=0)
        turned = rows.T
        spectra[pl.ds(j * parts, parts), :] = turned[0:parts]
        spectra[pl.ds((ROWS // 2 + j) * parts, parts), :] = turned[parts:2 * parts]
        if j < rest // 2:
            spectra[pl.ds((ROWS + j) * parts, 32), :] = turned[96:128]
        else:
            spectra[pl.ds((ROWS + j - rest // 2) * parts + 32, 16), :] = turned[96:112]

    for kb in range(kblocks):
        lanes = pl.ds(kb * LANES, LANES)
        re = spectra[pl.ds(kb * parts, fields, stride=2), :]
        im = spectra[pl.ds(kb * parts + 1, fields, stride=2), :]
        for pair in range(3 * groups // 2):
            real, imag = [], []
            for at in (2 * pair, 2 * pair + 1):
                c = mid_cos[pl.ds(at, 1), lanes]
                s = mid_sin[pl.ds(at, 1), lanes]
                real.append(re * c - im * s)
                imag.append(re * s + im * c)
            rows = pl.ds(pair * parts, parts)
            real_part[rows, lanes] = jnp.concatenate(real, axis=0).astype(jnp.bfloat16)
            imag_part[rows, lanes] = jnp.concatenate(imag, axis=0).astype(jnp.bfloat16)

    dims = (((1,), (1,)), ((), ()))
    even_sum = lax.dot_general(real_part[...], table_cos[...], dims, preferred_element_type=jnp.float32)
    odd_sum = lax.dot_general(imag_part[...], table_sin[...], dims, preferred_element_type=jnp.float32)
    ahead = even_sum - odd_sum
    behind = jnp.dot((even_sum + odd_sum).astype(jnp.bfloat16), flip, preferred_element_type=jnp.float32)
    lane = iota((1, HALF), 1)
    limit = count_smem[0, 0]

    def piece(tile, base, at, values):
        values = values[fields * (3 * tile + at):fields * (3 * tile + at + 1)]
        start = width * lax.rem(group + 1 + tile, groups) + base
        return jnp.where(lane + start < limit, values, 0.0).astype(jnp.bfloat16)

    sends = []
    for tile in range(groups):
        pieces = [piece(tile, 0, 0, behind), piece(tile, HALF, 0, ahead), piece(tile, 2 * HALF, 1, behind),
                  piece(tile, 3 * HALF, 1, ahead), piece(tile, 4 * HALF, 2, ahead)]
        result = jnp.concatenate(pieces, axis=1)
        if tile < groups - 1:
            tile_buf[tile] = result
            copy = pltpu.make_async_remote_copy(
                src_ref=tile_buf.at[tile], dst_ref=out_ref.at[group], send_sem=lev_send.at[tile],
                recv_sem=lev_recv.at[tile], device_id=(me, lax.rem(group + 1 + tile, groups)), device_id_type=MESH)
            copy.start()
            sends.append(copy)
        else:
            out_ref[group] = result
    bulk.wait_send()
    for tile, copy in enumerate(sends):
        copy.wait_send()
        sender = lax.rem(group + groups - 1 - tile, groups)
        pltpu.make_async_remote_copy(
            src_ref=tile_buf.at[tile], dst_ref=out_ref.at[sender], send_sem=lev_send.at[tile],
            recv_sem=lev_recv.at[tile], device_id=(me, sender), device_id_type=MESH).wait_recv()


def solution(mesh):
    waves, groups = mesh.shape["wave"], mesh.shape["lev"]

    def per_device(coeffs, legendre, wave_of_slot, lon_count):
        slots, parts, degrees = coeffs.shape
        lats = legendre.shape[1]
        fields = parts // 2
        width = 5120 // groups
        total = waves * slots
        centres = 3 * groups
        f32, bf16 = jnp.float32, jnp.bfloat16
        vmem = pl.BlockSpec(memory_space=pltpu.VMEM)
        hbm = pl.BlockSpec(memory_space=pltpu.HBM)
        dma = pltpu.SemaphoreType.DMA
        out = pl.pallas_call(
            functools.partial(kernel, waves, groups, slots, fields),
            out_shape=jax.ShapeDtypeStruct((groups, fields, width), bf16),
            in_specs=[hbm] * 4,
            out_specs=vmem,
            scratch_shapes=[
                pltpu.SMEM((1, 1), jnp.int32),
                pltpu.SMEM((total // LANES, LANES), jnp.int32),
                pltpu.VMEM((total // LANES, LANES), jnp.int32),
                pltpu.VMEM((slots, parts, degrees), bf16),
                pltpu.VMEM((slots, lats, degrees), bf16),
                pltpu.VMEM((waves * ROWS, LANES), f32),
                pltpu.VMEM((waves, ROWS, LANES), bf16),
                pltpu.VMEM((waves, ROWS, LANES), bf16),
                pltpu.VMEM((waves * ROWS, LANES), f32),
                pltpu.VMEM((slots // 2 * parts, LANES), f32),
                pltpu.VMEM((16, LANES), f32),
                pltpu.VMEM((16, total), f32), pltpu.VMEM((16, total), f32),
                pltpu.VMEM((16, total), f32), pltpu.VMEM((16, total), f32),
                pltpu.VMEM((16, total), f32), pltpu.VMEM((16, total), f32),
                pltpu.VMEM((HALF, total), bf16), pltpu.VMEM((HALF, total), bf16),
                pltpu.VMEM((centres * fields, total), bf16), pltpu.VMEM((centres * fields, total), bf16),
                pltpu.VMEM((groups - 1, fields, width), bf16),
                dma((3,)), dma((len(STEPS), 3)), dma((len(STEPS), 3)), dma, dma, dma((groups - 1,)), dma((groups - 1,)),
            ],
            compiler_params=pltpu.CompilerParams(
                collective_id=0, has_side_effects=True,
 vmem_limit_bytes=53 * 2 ** 20),
        )(coeffs, legendre, pltpu.with_memory_space_constraint(wave_of_slot.reshape(total // LANES, LANES), pltpu.HBM),
          lon_count.reshape(1, 1))
        return out.reshape(groups * fields, 1, width)

    return jax.shard_map(
        per_device,
        mesh=mesh,
        in_specs=(P("wave", "lev", None), P("wave", None, None), P(), P("wave")),
        out_specs=P(None, "wave", "lev"),
        check_vma=False,
    )
```

```python
import functools

import jax
import jax.numpy as jnp
from jax import lax
from jax.experimental import pallas as pl
from jax.experimental.pallas import tpu as pltpu
from jax.sharding import PartitionSpec as P

MESH = pl.DeviceIdType.MESH
LANES = 128
ROWS = 8
HALF = 256
STEPS = ((0, 4), (4, 4))
COS_POLY = (1.0, -4.934802055358887, 4.058712005615234, -1.335260272026062, 0.23532071709632874,
            -0.025785624980926514, 0.001904185046441853, -8.864672417985275e-05)
SIN_POLY = (3.1415927410125732, -5.167712688446045, 2.5501604080200195, -0.5992420315742493,
            0.08208133280277252, -0.00727477390319109, 0.0003950836544390768)


HOPS_Z = (0, 2, 4, 6, 8, 6, 4, 2)
HOPS_X = (0, 2, 4, 2)
WAVE_ORDER = sorted(range(64), key=lambda w: (HOPS_Z[w // 8] + HOPS_X[w // 2 % 4], -(w % 2), w))


def horner(poly, square):
    total = jnp.full_like(square, poly[-1])
    for value in poly[-2::-1]:
        total = total * square + value
    return total


def cos_sin(product, total, inverse):
    turns = jnp.round(product * (0.5 * inverse))
    part = (product - turns * (2.0 * total)) * inverse
    square = part * part
    return horner(COS_POLY, square), part * horner(SIN_POLY, square)


def iota(shape, dim):
    return lax.broadcasted_iota(jnp.int32, shape, dim)


def kernel(waves, groups, slots, fields,
           coef_hbm, leg_hbm, wave_hbm, count_hbm, out_ref,
           count_smem, wave_smem, wave_rows, coef, leg, packed, send_buf, recv_buf, arrived, spectra, wave_of_lane,
           fine_cos, fine_sin, coarse_cos, coarse_sin, mid_cos, mid_sin,
           table_cos, table_sin, real_part, imag_part, tile_buf,
           wave_sem, coef_sem, leg_sem, wave_send, wave_recv, lev_send, lev_recv):
    me = lax.axis_index("wave")
    group = lax.axis_index("lev")
    parts = 2 * fields
    degrees = coef.shape[2]
    kblocks = slots // 2
    width = out_ref.shape[2]

    rest = slots - 2 * ROWS

    def fetch(step):
        first, many = STEPS[step]
        starts = [first, ROWS + first] + ([2 * ROWS + first] if first < rest else [])
        for n, at in enumerate(starts):
            these = pl.ds(at, many)
            yield pltpu.make_async_copy(coef_hbm.at[these], coef.at[these], coef_sem.at[step, n])
            yield pltpu.make_async_copy(leg_hbm.at[these], leg.at[these], leg_sem.at[step, n])

    to_smem = pltpu.make_async_copy(wave_hbm, wave_smem, wave_sem.at[0])
    to_vmem = pltpu.make_async_copy(wave_hbm, wave_rows, wave_sem.at[1])
    to_count = pltpu.make_async_copy(count_hbm, count_smem, wave_sem.at[2])
    to_smem.start()
    to_vmem.start()
    to_count.start()
    for step in range(len(STEPS)):
        for copy in fetch(step):
            copy.start()

    barrier = pltpu.get_barrier_semaphore()

    for target in WAVE_ORDER:
        @pl.when(me != target)
        def _():
            pl.semaphore_signal(barrier, inc=1, device_id=(target, group), device_id_type=MESH)

    for j in range(1, groups):
        pl.semaphore_signal(barrier, inc=1, device_id=(me, lax.rem(group + j, groups)), device_id_type=MESH)

    to_smem.wait()
    to_vmem.wait()
    to_count.wait()

    degree = iota((1, degrees), 1)

    def number_of_slot(s):
        place = me * slots + s
        return wave_smem[place // LANES, lax.rem(place, LANES)]

    def legendre(s):
        limit = waves * slots - number_of_slot(s)
        mask = jnp.where(degree < limit, 1.0, 0.0).astype(jnp.bfloat16)
        return lax.dot_general(leg[s], coef[s] * mask, (((1,), (1,)), ((), ())),
                               preferred_element_type=jnp.float32)

    third = {}
    for r in range(ROWS):
        for step, (start, _) in enumerate(STEPS):
            if start == r:
                for copy in fetch(step):
                    copy.wait()
        first = legendre(r)
        second = legendre(ROWS + r)
        if r < rest:
            third[r] = legendre(2 * ROWS + r)
            tail = third[r][:, :32]
        else:
            tail = jnp.concatenate([third[r - rest][:, 32:], jnp.zeros((waves, 16), jnp.float32)], axis=1)
        packed[pl.ds(r, waves, stride=ROWS), :] = jnp.concatenate([first, second, tail], axis=1)
    send_buf[...] = packed[pl.ds(0, waves * ROWS), :].reshape(waves, ROWS, LANES).astype(jnp.bfloat16)
    recv_buf[me] = send_buf[me]

    pl.semaphore_wait(barrier, waves + groups - 2)

    for target in WAVE_ORDER:
        @pl.when(me != target)
        def _():
            pltpu.make_async_remote_copy(
                src_ref=send_buf.at[target], dst_ref=recv_buf.at[me], send_sem=wave_send, recv_sem=wave_recv,
                device_id=(target, group), device_id_type=MESH).start()

    numbers = wave_rows[...].astype(jnp.float32)
    high = jnp.floor(numbers * 0.125)
    low = numbers - 8.0 * high
    block_of = iota((16, LANES), 0)
    lane_of = iota((2 * waves, LANES), 0)
    gathered = jnp.zeros((64, 2 * waves), jnp.float32)
    for row in range(kblocks):
        slot_of = iota((1, LANES), 1) + row * LANES
        source = slot_of // slots
        slot_in = slot_of - slots * source
        picked = [jnp.where(slot_in == 2 * block_of + parity, value[row:row + 1], 0.0)
                  for value in (high, low) for parity in (0, 1)]
        spread = jnp.where((source == lane_of) | (source + waves == lane_of), 1.0, 0.0)
        gathered += lax.dot_general(jnp.concatenate(picked, axis=0).astype(jnp.bfloat16), spread.astype(jnp.bfloat16),
                                    (((1,), (1,)), ((), ())), preferred_element_type=jnp.float32)
    even = 8.0 * gathered[0:16] + gathered[32:48]
    odd = 8.0 * gathered[16:32] + gathered[48:64]
    wave_of_lane[...] = jnp.where(iota((16, LANES), 1) < waves, even, odd)

    count = count_smem[0, 0].astype(jnp.float32)
    total = jnp.full((1, LANES), count, jnp.float32)
    inverse = 1.0 / total
    row16 = iota((16, LANES), 0)
    fine_step = (2 * row16 + 1).astype(jnp.float32)
    coarse_step = (32 * row16).astype(jnp.float32)
    tile_at = (row16 >= 3).astype(jnp.int32) + (row16 >= 6).astype(jnp.int32) + (row16 >= 9).astype(jnp.int32)
    centre = row16 - 3 * tile_at
    tile_of = lax.rem(group + 1 + tile_at, groups)
    mid_step = (2 * width * tile_of + jnp.where(centre == 0, HALF * 2 - 1, jnp.where(centre == 1, HALF * 6 - 1, HALF * 8 - 1)))
    mid_step = mid_step.astype(jnp.float32)

    def tables(kb):
        lanes = pl.ds(pl.multiple_of(kb * LANES, LANES), LANES)
        m = jnp.broadcast_to(wave_of_lane[pl.ds(kb, 1), :], (16, LANES))
        fc, fs = cos_sin(m * fine_step, total, inverse)
        fine_cos[:, lanes] = fc
        fine_sin[:, lanes] = fs
        cc, cs = cos_sin(m * coarse_step, total, inverse)
        coarse_cos[:, lanes] = cc
        coarse_sin[:, lanes] = cs
        mc, ms = cos_sin(m * mid_step, total, inverse)
        factor = jnp.where(2.0 * m <= total - 1.0, jnp.where(m == 0.0, 1.0, 2.0), 0.0)
        mid_cos[:, lanes] = factor * mc
        mid_sin[:, lanes] = factor * ms
        for a in range(HALF // 16):
            ca = coarse_cos[pl.ds(a, 1), lanes]
            sa = coarse_sin[pl.ds(a, 1), lanes]
            table_cos[pl.ds(16 * a, 16), lanes] = (ca * fc - sa * fs).astype(jnp.bfloat16)
            table_sin[pl.ds(16 * a, 16), lanes] = (sa * fc + ca * fs).astype(jnp.bfloat16)

    pl.loop(0, kblocks)(tables)
    flip = jnp.where(iota((HALF, HALF), 0) + iota((HALF, HALF), 1) == HALF - 1, 1.0, 0.0).astype(jnp.bfloat16)

    bulk = pltpu.make_async_remote_copy(
        src_ref=send_buf.at[pl.ds(0, waves - 1)], dst_ref=recv_buf.at[pl.ds(0, waves - 1)],
        send_sem=wave_send, recv_sem=wave_recv, device_id=(me, group), device_id_type=MESH)
    bulk.wait_recv()

    arrived[pl.ds(0, waves * ROWS), :] = recv_buf[...].astype(jnp.float32).reshape(waves * ROWS, LANES)
    for j in range(ROWS // 2):
        rows = jnp.concatenate([arrived[pl.ds(2 * j, waves, stride=ROWS), :],
                                arrived[pl.ds(2 * j + 1, waves, stride=ROWS), :]], axis=0)
        turned = rows.T
        spectra[pl.ds(j * parts, parts), :] = turned[0:parts]
        spectra[pl.ds((ROWS // 2 + j) * parts, parts), :] = turned[parts:2 * parts]
        if j < rest // 2:
            spectra[pl.ds((ROWS + j) * parts, 32), :] = turned[96:128]
        else:
            spectra[pl.ds((ROWS + j - rest // 2) * parts + 32, 16), :] = turned[96:112]

    for kb in range(kblocks):
        lanes = pl.ds(kb * LANES, LANES)
        re = spectra[pl.ds(kb * parts, fields, stride=2), :]
        im = spectra[pl.ds(kb * parts + 1, fields, stride=2), :]
        for pair in range(3 * groups // 2):
            real, imag = [], []
            for at in (2 * pair, 2 * pair + 1):
                c = mid_cos[pl.ds(at, 1), lanes]
                s = mid_sin[pl.ds(at, 1), lanes]
                real.append(re * c - im * s)
                imag.append(re * s + im * c)
            rows = pl.ds(pair * parts, parts)
            real_part[rows, lanes] = jnp.concatenate(real, axis=0).astype(jnp.bfloat16)
            imag_part[rows, lanes] = jnp.concatenate(imag, axis=0).astype(jnp.bfloat16)

    dims = (((1,), (1,)), ((), ()))
    even_sum = lax.dot_general(real_part[...], table_cos[...], dims, preferred_element_type=jnp.float32)
    odd_sum = lax.dot_general(imag_part[...], table_sin[...], dims, preferred_element_type=jnp.float32)
    ahead = even_sum - odd_sum
    behind = jnp.dot((even_sum + odd_sum).astype(jnp.bfloat16), flip, preferred_element_type=jnp.float32)
    lane = iota((1, HALF), 1)
    limit = count_smem[0, 0]

    def piece(tile, base, at, values):
        values = values[fields * (3 * tile + at):fields * (3 * tile + at + 1)]
        start = width * lax.rem(group + 1 + tile, groups) + base
        return jnp.where(lane + start < limit, values, 0.0).astype(jnp.bfloat16)

    sends = []
    for tile in range(groups):
        pieces = [piece(tile, 0, 0, behind), piece(tile, HALF, 0, ahead), piece(tile, 2 * HALF, 1, behind),
                  piece(tile, 3 * HALF, 1, ahead), piece(tile, 4 * HALF, 2, ahead)]
        result = jnp.concatenate(pieces, axis=1)
        if tile < groups - 1:
            tile_buf[tile] = result
            copy = pltpu.make_async_remote_copy(
                src_ref=tile_buf.at[tile], dst_ref=out_ref.at[group], send_sem=lev_send.at[tile],
                recv_sem=lev_recv.at[tile], device_id=(me, lax.rem(group + 1 + tile, groups)), device_id_type=MESH)
            copy.start()
            sends.append(copy)
        else:
            out_ref[group] = result
    bulk.wait_send()
    for tile, copy in enumerate(sends):
        copy.wait_send()
        sender = lax.rem(group + groups - 1 - tile, groups)
        pltpu.make_async_remote_copy(
            src_ref=tile_buf.at[tile], dst_ref=out_ref.at[sender], send_sem=lev_send.at[tile],
            recv_sem=lev_recv.at[tile], device_id=(me, sender), device_id_type=MESH).wait_recv()


def solution(mesh):
    waves, groups = mesh.shape["wave"], mesh.shape["lev"]

    def per_device(coeffs, legendre, wave_of_slot, lon_count):
        slots, parts, degrees = coeffs.shape
        lats = legendre.shape[1]
        fields = parts // 2
        width = 5120 // groups
        total = waves * slots
        centres = 3 * groups
        f32, bf16 = jnp.float32, jnp.bfloat16
        vmem = pl.BlockSpec(memory_space=pltpu.VMEM)
        hbm = pl.BlockSpec(memory_space=pltpu.HBM)
        dma = pltpu.SemaphoreType.DMA
        out = pl.pallas_call(
            functools.partial(kernel, waves, groups, slots, fields),
            out_shape=jax.ShapeDtypeStruct((groups, fields, width), bf16),
            in_specs=[hbm] * 4,
            out_specs=vmem,
            scratch_shapes=[
                pltpu.SMEM((1, 1), jnp.int32),
                pltpu.SMEM((total // LANES, LANES), jnp.int32),
                pltpu.VMEM((total // LANES, LANES), jnp.int32),
                pltpu.VMEM((slots, parts, degrees), bf16),
                pltpu.VMEM((slots, lats, degrees), bf16),
                pltpu.VMEM((waves * ROWS + ROWS, LANES), f32),
                pltpu.VMEM((waves, ROWS, LANES), bf16),
                pltpu.VMEM((waves, ROWS, LANES), bf16),
                pltpu.VMEM((waves * ROWS + ROWS, LANES), f32),
                pltpu.VMEM((slots // 2 * parts + ROWS, LANES), f32),
                pltpu.VMEM((16, LANES), f32),
                pltpu.VMEM((16, total), f32), pltpu.VMEM((16, total), f32),
                pltpu.VMEM((16, total), f32), pltpu.VMEM((16, total), f32),
                pltpu.VMEM((16, total), f32), pltpu.VMEM((16, total), f32),
                pltpu.VMEM((HALF, total), bf16), pltpu.VMEM((HALF, total), bf16),
                pltpu.VMEM((centres * fields, total), bf16), pltpu.VMEM((centres * fields, total), bf16),
                pltpu.VMEM((groups - 1, fields, width), bf16),
                dma((3,)), dma((len(STEPS), 3)), dma((len(STEPS), 3)), dma, dma, dma((groups - 1,)), dma((groups - 1,)),
            ],
            compiler_params=pltpu.CompilerParams(
                collective_id=0, has_side_effects=True,
 vmem_limit_bytes=53 * 2 ** 20),
        )(coeffs, legendre, pltpu.with_memory_space_constraint(wave_of_slot.reshape(total // LANES, LANES), pltpu.HBM),
          lon_count.reshape(1, 1))
        return out.reshape(groups * fields, 1, width)

    return jax.shard_map(
        per_device,
        mesh=mesh,
        in_specs=(P("wave", "lev", None), P("wave", None, None), P(), P("wave")),
        out_specs=P(None, "wave", "lev"),
        check_vma=False,
    )
```
